32 devices in a mesh: sx: 8 (over z, y), sy: 4 (over x, core).
Axes of the slice: x: 2, y: 2, z: 4, core: 2. Of those that a mesh axis runs over, the one named last changes fastest.
Arguments:
- dual_ops: bfloat16 [8, 4, 2048, 2048], P('sx', 'sy'), may hold values from -0.028726213 to 1.0287262
- loads: float32 [8, 4, 2048, 128], P('sx', 'sy'), may hold values from -6 to 6
- kernel_basis: bfloat16 [8, 4, 64, 2048], P('sx', 'sy'), may hold values from -0.13183594 to 0.13183594
- coarse_inverse: bfloat16 [8, 4, 256, 512], P('sx', 'sy'), may hold values from -1 to 1
Outputs:
- multipliers: float32 [8, 4, 2048, 128], P('sx', 'sy')
The draws below stay inside these ranges and needn't reach their ends.
All inputs are finite; a program needn't handle non-finite values.
Results may differ from the reference program's by a relative error of at most 0.0085.
Values may be sent and summed in bfloat16 or wider, within the bound.
A program may use at most 64 MiB of HBM per device.

```python
import jax
import jax.numpy as jnp
from jax import lax

IFACE = 2048
KB = 64
LOADS = 128
ITERS = 3
N_SX = 8
N_SY = 4


def draw_dual_ops(key, part):
    noise_key = jax.random.fold_in(key, 11)
    shape = (N_SX, N_SY, IFACE, IFACE)
    noise = jnp.clip(jax.random.normal(noise_key, shape, jnp.float32), -4.0, 4.0)
    identity = jnp.eye(IFACE, dtype=jnp.float32)
    return (identity + 0.3 / IFACE ** 0.5 * noise).astype(jnp.bfloat16)


def draw_coarse_inverse(key, part):
    noise_key = jax.random.fold_in(key, 23)
    shape = (N_SX, N_SY, KB * N_SY, KB * N_SX)
    row_grid = jnp.arange(N_SX, dtype=jnp.int32)[:, None, None, None]
    col_grid = jnp.arange(N_SY, dtype=jnp.int32)[None, :, None, None]
    inner = jnp.arange(KB * N_SY, dtype=jnp.int32)[None, None, :, None]
    outer = jnp.arange(KB * N_SX, dtype=jnp.int32)[None, None, None, :]
    piece_row = inner // KB
    piece_col = outer // KB
    diagonal = (row_grid == piece_col) & (col_grid == piece_row) & (inner % KB == outer % KB)
    spike = piece_row == (piece_col + row_grid + col_grid) % N_SY
    noise = jnp.clip(jax.random.normal(noise_key, shape, jnp.float32), -4.0, 4.0)
    scale = jnp.where(spike, 0.3 / KB ** 0.5, 0.5 / (KB * N_SX * N_SY) ** 0.5)
    return (0.5 * diagonal.astype(jnp.float32) + scale * noise).astype(jnp.bfloat16)


def level_of(key, extent, split, low, high):
    def one(position, shards_of):
        steps = jax.random.uniform(jax.random.fold_in(jax.random.fold_in(key, 6), position), (shards_of,), jnp.float32, low / len(split), high / len(split))
        return jnp.repeat(jnp.exp(steps), extent[position] // shards_of).reshape((-1,) + (1,) * (len(extent) - position - 1))

    loudness = one(*split[0])
    for cut in split[1:]:
        loudness = loudness * one(*cut)
    return loudness


def centred(stream_key, extent, scale, reach, split=(), kind=jnp.bfloat16):
    factor_of = level_of(stream_key, extent, split, -0.22, 0.18) if split else 1.0
    drawn = jax.random.normal(stream_key, extent, jnp.float32) * scale * factor_of
    return jnp.minimum(jnp.maximum(drawn, -reach), reach).astype(kind)


def setup_inputs(seed: int = 0) -> dict:
    key_list = jax.random.split(jax.random.key(seed), 5)
    dual_ops = draw_dual_ops(jax.random.fold_in(key_list[4], 71), 0)
    loads = centred(key_list[1], (N_SX, N_SY, IFACE, LOADS), 1.0, 6.0, ((0, 8), (1, 4)), jnp.float32)
    kernel_basis = centred(key_list[2], (N_SX, N_SY, KB, IFACE), (1.0 / IFACE ** 0.5), 0.13183594, ((0, 8), (1, 4)))
    coarse_inverse = draw_coarse_inverse(jax.random.fold_in(key_list[4], 71), 0)
    return {"dual_ops": dual_ops, "loads": loads, "kernel_basis": kernel_basis, "coarse_inverse": coarse_inverse}


damping = 0.5


def face_sum(values):
    width = values.shape[2] // 4
    north = values[:, :, :width]
    south = values[:, :, width:2 * width]
    west = values[:, :, 2 * width:3 * width]
    east = values[:, :, 3 * width:]
    zero_row = jnp.zeros_like(south[:1])
    from_north = jnp.concatenate([zero_row, south[:-1]], axis=0)
    from_south = jnp.concatenate([north[1:], zero_row], axis=0)
    zero_col = jnp.zeros_like(east[:, :1])
    from_west = jnp.concatenate([zero_col, east[:, :-1]], axis=1)
    from_east = jnp.concatenate([west[:, 1:], zero_col], axis=1)
    return jnp.concatenate([north - from_north, south - from_south, west - from_west, east - from_east], axis=2)


def coarse_apply(coarse_inverse, coarse_in):
    nx, ny, kb, nload = coarse_in.shape
    columns = jnp.transpose(coarse_in, (1, 0, 2, 3)).reshape(ny, nx * kb, nload).astype(jnp.float32)

    def row_of(tiles):
        return jnp.einsum('bij,bjl->il', tiles.astype(jnp.float32), columns, precision=lax.Precision.HIGHEST)

    result = lax.map(row_of, coarse_inverse)
    return result.reshape(nx, ny, kb, nload)


def reference(dual_ops, loads, kernel_basis, coarse_inverse):
    nx, ny, nrow, nload = loads.shape
    flat_ops = dual_ops.reshape(nx * ny, nrow, nrow)
    basis_wide = kernel_basis.astype(jnp.float32)
    multipliers = jnp.zeros(loads.shape, jnp.float32)
    for step in range(ITERS):
        rounded = multipliers.astype(jnp.bfloat16).reshape(nx * ny, nrow, nload)
        product = lax.map(lambda pair: jnp.dot(pair[0], pair[1], preferred_element_type=jnp.float32), (flat_ops, rounded))
        product = product.reshape(loads.shape)
        residual = face_sum(loads - product)
        resid_half = lax.optimization_barrier(residual.astype(jnp.bfloat16))
        coarse_in = jnp.einsum('abkn,abnl->abkl', basis_wide, resid_half.astype(jnp.float32), precision=lax.Precision.HIGHEST).astype(jnp.bfloat16)
        coarse_out = lax.optimization_barrier(coarse_apply(coarse_inverse, coarse_in).astype(jnp.bfloat16))
        back = jnp.einsum('abkn,abkl->abnl', basis_wide, coarse_out.astype(jnp.float32), precision=lax.Precision.HIGHEST)
        multipliers = multipliers + damping * (residual - face_sum(back))
    return multipliers
```

```python
import functools

import jax
import jax.numpy as jnp
from jax import lax
from jax.experimental import pallas as pl
from jax.experimental.pallas import tpu as pltpu
from jax.sharding import PartitionSpec as P

ITERS = 3
DAMPING = 0.5
MESH = pl.DeviceIdType.MESH
F32 = jnp.float32
BF16 = jnp.bfloat16


def iterate(
    nx,
    ny,
    dual_hbm,
    loads,
    basis,
    tile,
    out,
    dual,
    faces,
    halo,
    beside_basis,
    spread,
    half,
    resid,
    gathered,
    slices,
    arrived,
    coarse,
    coarse_near,
    dual_sem,
    face_send,
    face_recv,
    basis_send,
    basis_recv,
    gather_send,
    gather_recv,
    slice_send,
    slice_recv,
    near_send,
    near_recv,
):
    a, b = lax.axis_index("sx"), lax.axis_index("sy")
    width = loads.shape[0] // 4
    modes = basis.shape[0]
    peers = ((a - 1, b), (a + 1, b), (a, b - 1), (a, b + 1))
    present = (a > 0, a < nx - 1, b > 0, b < ny - 1)
    opposite = (1, 0, 3, 2)

    dual_copy = pltpu.make_async_copy(dual_hbm, dual, dual_sem)
    dual_copy.start()

    barrier = pltpu.get_barrier_semaphore()
    for k in range(1, nx):
        pl.semaphore_signal(
            barrier, inc=1, device_id=(lax.rem(a + k, nx), b), device_id_type=MESH
        )
    for k in range(1, ny):
        pl.semaphore_signal(
            barrier, inc=1, device_id=(a, lax.rem(b + k, ny)), device_id_type=MESH
        )

    def rows(f):
        return pl.ds(f * width, width)

    for f in range(4):
        faces[0, f] = loads[rows(f), :].astype(BF16)

        @pl.when(jnp.logical_not(present[f]))
        def _():
            for step in range(ITERS):
                halo[step, f] = jnp.zeros(halo.shape[2:], BF16)
                coarse_near[step, f] = jnp.zeros(coarse_near.shape[2:], BF16)
            beside_basis[f] = jnp.zeros(beside_basis.shape[1:], BF16)

    pl.semaphore_wait(barrier, nx - 1 + ny - 1)

    def face_copy(step, f, slot):
        return pltpu.make_async_remote_copy(
            src_ref=faces.at[step, f],
            dst_ref=halo.at[step, slot],
            send_sem=face_send.at[step, f],
            recv_sem=face_recv.at[step, slot],
            device_id=peers[f],
            device_id_type=MESH,
        )

    def basis_copy(f, slot):
        return pltpu.make_async_remote_copy(
            src_ref=basis.at[:, rows(f)],
            dst_ref=beside_basis.at[slot],
            send_sem=basis_send.at[f],
            recv_sem=basis_recv.at[slot],
            device_id=peers[f],
            device_id_type=MESH,
        )

    def near_copy(step, f, slot):
        return pltpu.make_async_remote_copy(
            src_ref=coarse.at[step],
            dst_ref=coarse_near.at[step, slot],
            send_sem=near_send.at[step, f],
            recv_sem=near_recv.at[step, slot],
            device_id=peers[f],
            device_id_type=MESH,
        )

    def gather_copy(step, k):
        return pltpu.make_async_remote_copy(
            src_ref=gathered.at[step, a],
            dst_ref=gathered.at[step, a],
            send_sem=gather_send.at[step, k],
            recv_sem=gather_recv.at[step, k],
            device_id=(lax.rem(a + k, nx), b),
            device_id_type=MESH,
        )

    def slice_copy(step, k):
        target = lax.rem(b + k, ny)
        return pltpu.make_async_remote_copy(
            src_ref=slices.at[step, target],
            dst_ref=arrived.at[step, k],
            send_sem=slice_send.at[step, k],
            recv_sem=slice_recv.at[step, k],
            device_id=(a, target),
            device_id_type=MESH,
        )

    def each(make, f, what):
        @pl.when(present[f])
        def _():
            getattr(make(f, opposite[f]), what)()

    def expect(make, f):
        @pl.when(present[f])
        def _():
            make(f, f).wait_recv()

    for step in range(ITERS):
        here = functools.partial(face_copy, step)
        near = functools.partial(near_copy, step)
        for f in range(4):
            if step:

                @pl.loop(0, 2)
                def _(part):
                    span = width // 2
                    start = pl.multiple_of(f * width + part * span, span)
                    local = loads[pl.ds(start, span), :] - jnp.dot(
                        dual[pl.ds(start, span), :], half[...], preferred_element_type=F32
                    )
                    resid[pl.ds(start, span), :] = local
                    inner = pl.multiple_of(part * span, span)
                    faces[step, f, pl.ds(inner, span), :] = local.astype(BF16)

            each(here, f, "start")
        if step == 0:
            for f in range(4):
                each(basis_copy, f, "start")
        total = jnp.zeros((modes, loads.shape[1]), F32)
        for f in range(4):
            expect(here, f)
            own = resid if step else loads
            value = own[rows(f), :] - halo[step, f].astype(F32)
            resid[rows(f), :] = value
            total += jnp.dot(
                basis[:, rows(f)], value.astype(BF16), preferred_element_type=F32
            )
        gathered[step, a] = total.astype(BF16)
        for k in range(1, nx):
            gather_copy(step, k).start()
        if step == 0:
            dual_copy.wait()
            for f in range(4):
                expect(basis_copy, f)
                pair = jnp.concatenate([basis[:, rows(f)], -beside_basis[f]], axis=0)
                spread[rows(f), :] = pair.astype(F32).T.astype(BF16)
        for k in range(1, nx):
            gather_copy(step, k).wait_recv()
        column = gathered[step].reshape(nx * modes, loads.shape[1])
        partial = jnp.dot(tile[...], column, preferred_element_type=F32)
        slices[step] = partial.reshape(ny, modes, loads.shape[1])
        for k in range(1, ny):
            slice_copy(step, k).start()
        total = slices[step, b]
        for k in range(1, ny):
            slice_copy(step, k).wait_recv()
            total += arrived[step, k]
        coarse[step] = total.astype(BF16)
        for f in range(4):
            each(near, f, "start")
        for f in range(4):
            expect(near, f)
            stacked = jnp.concatenate([coarse[step], coarse_near[step, f]], axis=0)
            correction = jnp.dot(spread[rows(f), :], stacked, preferred_element_type=F32)
            value = DAMPING * (resid[rows(f), :] - correction)
            if step:
                value += out[rows(f), :]
            out[rows(f), :] = value
            if step < ITERS - 1:
                half[rows(f), :] = value.astype(BF16)

    for f in range(4):
        each(basis_copy, f, "wait_send")
        for step in range(ITERS):
            each(functools.partial(face_copy, step), f, "wait_send")
            each(functools.partial(near_copy, step), f, "wait_send")
    for step in range(ITERS):
        for k in range(1, nx):
            gather_copy(step, k).wait_send()
        for k in range(1, ny):
            slice_copy(step, k).wait_send()


def local(nx, ny, dual_ops, loads, kernel_basis, coarse_inverse):
    n, cols = loads.shape[2:]
    modes = kernel_basis.shape[2]
    width = n // 4
    vmem = pl.BlockSpec(memory_space=pltpu.VMEM)
    dma = pltpu.SemaphoreType.DMA
    result = pl.pallas_call(
        functools.partial(iterate, nx, ny),
        out_shape=jax.ShapeDtypeStruct((n, cols), F32),
        in_specs=[pl.BlockSpec(memory_space=pl.ANY), vmem, vmem, vmem],
        out_specs=vmem,
        scratch_shapes=[
            pltpu.VMEM((n, n), BF16),
            pltpu.VMEM((ITERS, 4, width, cols), BF16),
            pltpu.VMEM((ITERS, 4, width, cols), BF16),
            pltpu.VMEM((4, modes, width), BF16),
            pltpu.VMEM((n, 2 * modes), BF16),
            pltpu.VMEM((n, cols), BF16),
            pltpu.VMEM((n, cols), F32),
            pltpu.VMEM((ITERS, nx, modes, cols), BF16),
            pltpu.VMEM((ITERS, ny, modes, cols), F32),
            pltpu.VMEM((ITERS, ny, modes, cols), F32),
            pltpu.VMEM((ITERS, modes, cols), BF16),
            pltpu.VMEM((ITERS, 4, modes, cols), BF16),
            dma(()),
            dma((ITERS, 4)),
            dma((ITERS, 4)),
            dma((4,)),
            dma((4,)),
            dma((ITERS, nx)),
            dma((ITERS, nx)),
            dma((ITERS, ny)),
            dma((ITERS, ny)),
            dma((ITERS, 4)),
            dma((ITERS, 4)),
        ],
        compiler_params=pltpu.CompilerParams(
            collective_id=0, has_side_effects=True, vmem_limit_bytes=40 * 2**20
        ),
    )(dual_ops[0, 0], loads[0, 0], kernel_basis[0, 0], coarse_inverse[0, 0])
    return result[None, None]


def solution(mesh):
    placed = P("sx", "sy", None, None)
    return jax.shard_map(
        functools.partial(local, mesh.shape["sx"], mesh.shape["sy"]),
        mesh=mesh,
        in_specs=(placed,) * 4,
        out_specs=placed,
        check_vma=False,
    )
```

```python
import functools

import jax
import jax.numpy as jnp
from jax import lax
from jax.experimental import pallas as pl
from jax.experimental.pallas import tpu as pltpu
from jax.sharding import PartitionSpec as P

ITERS = 3
DAMPING = 0.5
MESH = pl.DeviceIdType.MESH
F32 = jnp.float32
BF16 = jnp.bfloat16


def iterate(
    nx,
    ny,
    dual_hbm,
    loads_hbm,
    basis_hbm,
    tile_hbm,
    out,
    dual,
    loads,
    basis,
    tile,
    faces,
    halo,
    beside_basis,
    spread,
    spread_rows,
    image,
    gram,
    half,
    resid,
    base,
    base_modes,
    offered,
    offers,
    gathered,
    slices,
    arrived,
    coarse,
    coarse_near,
    local_sem,
    face_send,
    face_recv,
    basis_send,
    basis_recv,
    offer_send,
    offer_recv,
    gather_send,
    gather_recv,
    slice_send,
    slice_recv,
    near_send,
    near_recv,
):
    a, b = lax.axis_index("sx"), lax.axis_index("sy")
    n, cols = loads.shape
    width = n // 4
    modes = basis.shape[0]
    peers = ((a - 1, b), (a + 1, b), (a, b - 1), (a, b + 1))
    present = (a > 0, a < nx - 1, b > 0, b < ny - 1)
    opposite = (1, 0, 3, 2)

    loads_copy = pltpu.make_async_copy(loads_hbm, loads, local_sem.at[0])
    basis_load = pltpu.make_async_copy(basis_hbm, basis, local_sem.at[1])
    dual_copy = pltpu.make_async_copy(dual_hbm, dual, local_sem.at[2])
    tile_copy = pltpu.make_async_copy(tile_hbm, tile, local_sem.at[3])
    loads_copy.start()
    basis_load.start()
    dual_copy.start()
    tile_copy.start()

    barrier = pltpu.get_barrier_semaphore()
    for k in range(1, nx):
        pl.semaphore_signal(
            barrier, inc=1, device_id=(lax.rem(a + k, nx), b), device_id_type=MESH
        )
    for k in range(1, ny):
        pl.semaphore_signal(
            barrier, inc=1, device_id=(a, lax.rem(b + k, ny)), device_id_type=MESH
        )

    def rows(f):
        return pl.ds(f * width, width)

    for f in range(4):

        @pl.when(jnp.logical_not(present[f]))
        def _():
            for step in range(ITERS):
                halo[step, f] = jnp.zeros(halo.shape[2:], BF16)
                coarse_near[step, f] = jnp.zeros(coarse_near.shape[2:], BF16)
                offers[step, f] = jnp.zeros(offers.shape[2:], BF16)
            beside_basis[f] = jnp.zeros(beside_basis.shape[1:], BF16)

    loads_copy.wait()
    for f in range(4):
        faces[0, f] = loads[rows(f), :].astype(BF16)
    basis_load.wait()

    pl.semaphore_wait(barrier, nx - 1 + ny - 1)

    def to_face(src, dst, sends, recvs, f, slot):
        return pltpu.make_async_remote_copy(
            src_ref=src,
            dst_ref=dst,
            send_sem=sends,
            recv_sem=recvs,
            device_id=peers[f],
            device_id_type=MESH,
        )

    def face_copy(step, f, slot):
        return to_face(
            faces.at[step, f],
            halo.at[step, slot],
            face_send.at[step, f],
            face_recv.at[step, slot],
            f,
            slot,
        )

    def basis_copy(step, f, slot):
        return to_face(
            basis.at[:, rows(f)],
            beside_basis.at[slot],
            basis_send.at[f],
            basis_recv.at[slot],
            f,
            slot,
        )

    def offer_copy(step, f, slot):
        return to_face(
            offered.at[step, f],
            offers.at[step, slot],
            offer_send.at[step, f],
            offer_recv.at[step, slot],
            f,
            slot,
        )

    def near_copy(step, f, slot):
        return to_face(
            coarse.at[step],
            coarse_near.at[step, slot],
            near_send.at[step, f],
            near_recv.at[step, slot],
            f,
            slot,
        )

    def gather_copy(step, k):
        return pltpu.make_async_remote_copy(
            src_ref=gathered.at[step, a],
            dst_ref=gathered.at[step, a],
            send_sem=gather_send.at[step, k],
            recv_sem=gather_recv.at[step, k],
            device_id=(lax.rem(a + k, nx), b),
            device_id_type=MESH,
        )

    def slice_copy(step, k):
        target = lax.rem(b + k, ny)
        return pltpu.make_async_remote_copy(
            src_ref=slices.at[step, target],
            dst_ref=arrived.at[step, k],
            send_sem=slice_send.at[step, k],
            recv_sem=slice_recv.at[step, k],
            device_id=(a, target),
            device_id_type=MESH,
        )

    def send(make, step, f):
        @pl.when(present[f])
        def _():
            make(step, f, opposite[f]).start()

    def sent(make, step, f):
        @pl.when(present[f])
        def _():
            make(step, f, opposite[f]).wait_send()

    def expect(make, step, f):
        @pl.when(present[f])
        def _():
            make(step, f, f).wait_recv()

    def dot(x, y):
        return jnp.dot(x, y, preferred_element_type=F32)

    def with_near(step):
        return jnp.concatenate([coarse[step]] + [coarse_near[step, f] for f in range(4)], axis=0)

    def share(step, total):
        gathered[step, a] = total.astype(BF16)
        for k in range(1, nx):
            gather_copy(step, k).start()

    def spread_tiles(step):
        for k in range(1, nx):
            gather_copy(step, k).wait_recv()
        partial = dot(tile[...], gathered[step].reshape(nx * modes, cols))
        slices[step] = partial.astype(BF16).reshape(ny, modes, cols)
        for k in range(1, ny):
            slice_copy(step, k).start()

    def finish_coarse(step):
        total = slices[step, b].astype(F32)
        for k in range(1, ny):
            slice_copy(step, k).wait_recv()
            total += arrived[step, k].astype(F32)
        coarse[step] = total.astype(BF16)
        for f in range(4):
            send(near_copy, step, f)

    def apply_dual(first, count):
        span = width // 2

        @pl.loop(first, first + count)
        def _(part):
            start = pl.multiple_of(part * span, span)
            base[pl.ds(start, span), :] = loads[pl.ds(start, span), :] - dot(
                dual[pl.ds(start, span), :], half[...]
            )

    def to_modes(read):
        own = jnp.zeros((modes, cols), F32)
        for f in range(4):
            both = dot(spread_rows[f], read(f).astype(BF16))
            own += both[:modes]
            base_modes[pl.ds((f + 1) * modes, modes), :] = both[modes:]
        base_modes[pl.ds(0, modes), :] = own

    def correct(step, f):
        stacked = jnp.concatenate([coarse[step], coarse_near[step, f]], axis=0)
        return DAMPING * dot(spread[rows(f), :], stacked)

    for f in range(4):
        send(face_copy, 0, f)
    for f in range(4):
        send(basis_copy, 0, f)
    total = jnp.zeros((modes, cols), F32)
    for f in range(4):
        expect(face_copy, 0, f)
        value = loads[rows(f), :] - halo[0, f].astype(F32)
        total += dot(basis[:, rows(f)], value.astype(BF16))
        out[rows(f), :] = DAMPING * value
        half[rows(f), :] = (DAMPING * value).astype(BF16)
    share(0, total)
    for f in range(4):
        expect(basis_copy, 0, f)
        pair = jnp.concatenate([basis[:, rows(f)], -beside_basis[f]], axis=0)
        spread_rows[f] = pair
        spread[rows(f), :] = pair.astype(F32).T.astype(BF16)
    dual_copy.wait()
    tile_copy.wait()
    spread_tiles(0)

    @pl.loop(0, 8)
    def _(part):
        span = width // 2
        start = pl.multiple_of(part * span, span)
        own = jnp.zeros((span, modes), F32)
        columns = []
        for f in range(4):
            both = dot(dual[pl.ds(start, span), rows(f)], spread[rows(f), :])
            own += both[:, :modes]
            columns.append(both[:, modes:])
        image[pl.ds(start, span), :] = jnp.concatenate([own] + columns, axis=1).astype(BF16)

    finish_coarse(0)
    own = jnp.zeros((modes, 5 * modes), F32)
    for f in range(4):
        both = dot(spread_rows[f], image[rows(f), :])
        own += both[:modes]
        gram[pl.ds((f + 1) * modes, modes), :] = both[modes:].astype(BF16)
    gram[pl.ds(0, modes), :] = own.astype(BF16)
    apply_dual(0, 8)
    to_modes(lambda f: base[rows(f), :])

    for step in range(1, ITERS):
        for f in range(4):
            expect(near_copy, step - 1, f)
        stack = with_near(step - 1)
        total_modes = base_modes[...] + DAMPING * dot(gram[...], stack)
        for f in range(4):
            offered[step, f] = total_modes[(f + 1) * modes : (f + 2) * modes].astype(BF16)
            send(offer_copy, step, f)
        for f in range(4):
            value = base[rows(f), :] + DAMPING * dot(image[rows(f), :], stack)
            resid[rows(f), :] = value
            faces[step, f] = value.astype(BF16)
            send(face_copy, step, f)
        total = total_modes[:modes]
        for f in range(4):
            expect(offer_copy, step, f)
            total += offers[step, f].astype(F32)
        share(step, total)
        for f in range(4):
            out[rows(f), :] = out[rows(f), :] - correct(step - 1, f)
        spread_tiles(step)
        for f in range(4):
            expect(face_copy, step, f)
            value = out[rows(f), :] + DAMPING * (resid[rows(f), :] - halo[step, f].astype(F32))
            out[rows(f), :] = value
            if step < ITERS - 1:
                half[rows(f), :] = value.astype(BF16)
        if step < ITERS - 1:
            apply_dual(0, 4)
        finish_coarse(step)
        if step < ITERS - 1:
            apply_dual(4, 4)
            to_modes(lambda f: base[rows(f), :])

    for f in range(4):
        expect(near_copy, ITERS - 1, f)
        out[rows(f), :] = out[rows(f), :] - correct(ITERS - 1, f)

    for f in range(4):
        sent(basis_copy, 0, f)
        for step in range(ITERS):
            sent(face_copy, step, f)
            sent(near_copy, step, f)
            if step:
                sent(offer_copy, step, f)
    for step in range(ITERS):
        for k in range(1, nx):
            gather_copy(step, k).wait_send()
        for k in range(1, ny):
            slice_copy(step, k).wait_send()


def local(nx, ny, dual_ops, loads, kernel_basis, coarse_inverse):
    n, cols = loads.shape[2:]
    modes = kernel_basis.shape[2]
    width = n // 4
    dma = pltpu.SemaphoreType.DMA
    result = pl.pallas_call(
        functools.partial(iterate, nx, ny),
        out_shape=jax.ShapeDtypeStruct((n, cols), F32),
        in_specs=[pl.BlockSpec(memory_space=pl.ANY)] * 4,
        out_specs=pl.BlockSpec(memory_space=pltpu.VMEM),
        scratch_shapes=[
            pltpu.VMEM((n, n), BF16),
            pltpu.VMEM((n, cols), F32),
            pltpu.VMEM((modes, n), BF16),
            pltpu.VMEM(coarse_inverse.shape[2:], BF16),
            pltpu.VMEM((ITERS, 4, width, cols), BF16),
            pltpu.VMEM((ITERS, 4, width, cols), BF16),
            pltpu.VMEM((4, modes, width), BF16),
            pltpu.VMEM((n, 2 * modes), BF16),
            pltpu.VMEM((4, 2 * modes, width), BF16),
            pltpu.VMEM((n, 5 * modes), BF16),
            pltpu.VMEM((5 * modes, 5 * modes), BF16),
            pltpu.VMEM((n, cols), BF16),
            pltpu.VMEM((n, cols), F32),
            pltpu.VMEM((n, cols), F32),
            pltpu.VMEM((5 * modes, cols), F32),
            pltpu.VMEM((ITERS, 4, modes, cols), BF16),
            pltpu.VMEM((ITERS, 4, modes, cols), BF16),
            pltpu.VMEM((ITERS, nx, modes, cols), BF16),
            pltpu.VMEM((ITERS, ny, modes, cols), BF16),
            pltpu.VMEM((ITERS, ny, modes, cols), BF16),
            pltpu.VMEM((ITERS, modes, cols), BF16),
            pltpu.VMEM((ITERS, 4, modes, cols), BF16),
            dma((4,)),
            dma((ITERS, 4)),
            dma((ITERS, 4)),
            dma((4,)),
            dma((4,)),
            dma((ITERS, 4)),
            dma((ITERS, 4)),
            dma((ITERS, nx)),
            dma((ITERS, nx)),
            dma((ITERS, ny)),
            dma((ITERS, ny)),
            dma((ITERS, 4)),
            dma((ITERS, 4)),
        ],
        compiler_params=pltpu.CompilerParams(
            collective_id=0, has_side_effects=True, vmem_limit_bytes=58 * 2**20
        ),
    )(dual_ops[0, 0], loads[0, 0], kernel_basis[0, 0], coarse_inverse[0, 0])
    return result[None, None]


def solution(mesh):
    placed = P("sx", "sy", None, None)
    return jax.shard_map(
        functools.partial(local, mesh.shape["sx"], mesh.shape["sy"]),
        mesh=mesh,
        in_specs=(placed,) * 4,
        out_specs=placed,
        check_vma=False,
    )
```

```python
import functools

import jax
import jax.numpy as jnp
from jax import lax
from jax.experimental import pallas as pl
from jax.experimental.pallas import tpu as pltpu
from jax.sharding import PartitionSpec as P

ITERS = 3
DAMPING = 0.5
MESH = pl.DeviceIdType.MESH
F32 = jnp.float32
BF16 = jnp.bfloat16


def iterate(
    nx,
    ny,
    dual_hbm,
    loads_hbm,
    basis_hbm,
    tile_hbm,
    out,
    dual,
    loads,
    basis,
    tile,
    faces,
    halo,
    beside_basis,
    spread,
    spread_rows,
    image,
    gram,
    gram_near,
    half,
    resid,
    base,
    base_modes,
    offered,
    offers,
    gathered,
    slices,
    arrived,
    coarse,
    coarse_near,
    local_sem,
    face_send,
    face_recv,
    basis_send,
    basis_recv,
    offer_send,
    offer_recv,
    gather_send,
    gather_recv,
    slice_send,
    slice_recv,
    near_send,
    near_recv,
    gram_send,
    gram_recv,
):
    a, b = lax.axis_index("sx"), lax.axis_index("sy")
    n, cols = loads.shape
    width = n // 4
    modes = basis.shape[0]
    peers = ((a - 1, b), (a + 1, b), (a, b - 1), (a, b + 1))
    present = (a > 0, a < nx - 1, b > 0, b < ny - 1)
    opposite = (1, 0, 3, 2)
    compass = ((-1, 0), (1, 0), (0, -1), (0, 1))
    diagonal = ((-1, -1), (-1, 1), (1, -1), (1, 1))
    straight = ((-2, 0), (2, 0), (0, -2), (0, 2))

    def inside(offset):
        row, column = a + offset[0], b + offset[1]
        return (row >= 0) & (row < nx) & (column >= 0) & (column < ny)

    def around(step):
        return compass if step == ITERS - 1 else compass + diagonal + straight

    loads_copy = pltpu.make_async_copy(loads_hbm, loads, local_sem.at[0])
    basis_load = pltpu.make_async_copy(basis_hbm, basis, local_sem.at[1])
    dual_copy = pltpu.make_async_copy(dual_hbm, dual, local_sem.at[2])
    tile_copy = pltpu.make_async_copy(tile_hbm, tile, local_sem.at[3])
    loads_copy.start()
    basis_load.start()
    dual_copy.start()
    tile_copy.start()

    barrier = pltpu.get_barrier_semaphore()
    for k in range(1, nx):
        pl.semaphore_signal(
            barrier, inc=1, device_id=(lax.rem(a + k, nx), b), device_id_type=MESH
        )
    for k in range(1, ny):
        pl.semaphore_signal(
            barrier, inc=1, device_id=(a, lax.rem(b + k, ny)), device_id_type=MESH
        )

    greeted = jnp.int32(nx - 1 + ny - 1)
    for offset in diagonal:
        greeted += inside(offset).astype(jnp.int32)

        @pl.when(inside(offset))
        def _():
            pl.semaphore_signal(
                barrier,
                inc=1,
                device_id=(a + offset[0], b + offset[1]),
                device_id_type=MESH,
            )

    def rows(f):
        return pl.ds(f * width, width)

    for offset in compass + diagonal + straight:

        @pl.when(jnp.logical_not(inside(offset)))
        def _():
            for step in range(ITERS):
                coarse_near[step, 2 + offset[0], 2 + offset[1]] = jnp.zeros((modes, cols), BF16)

    for f in range(4):

        @pl.when(jnp.logical_not(present[f]))
        def _():
            for step in range(ITERS):
                halo[step, f] = jnp.zeros(halo.shape[2:], BF16)
                offers[step, f] = jnp.zeros(offers.shape[2:], BF16)
            beside_basis[f] = jnp.zeros(beside_basis.shape[1:], BF16)
            gram_near[f] = jnp.zeros(gram_near.shape[1:], BF16)

    loads_copy.wait()
    for f in range(4):
        faces[0, f] = loads[rows(f), :].astype(BF16)
    basis_load.wait()

    pl.semaphore_wait(barrier, greeted)

    def to_face(src, dst, sends, recvs, f, slot):
        return pltpu.make_async_remote_copy(
            src_ref=src,
            dst_ref=dst,
            send_sem=sends,
            recv_sem=recvs,
            device_id=peers[f],
            device_id_type=MESH,
        )

    def face_copy(step, f, slot):
        return to_face(
            faces.at[step, f],
            halo.at[step, slot],
            face_send.at[step, f],
            face_recv.at[step, slot],
            f,
            slot,
        )

    def basis_copy(step, f, slot):
        return to_face(
            basis.at[:, rows(f)],
            beside_basis.at[slot],
            basis_send.at[f],
            basis_recv.at[slot],
            f,
            slot,
        )

    def offer_copy(step, f, slot):
        return to_face(
            offered.at[step, f],
            offers.at[step, slot],
            offer_send.at[step, f],
            offer_recv.at[step, slot],
            f,
            slot,
        )

    def gram_copy(step, f, slot):
        return to_face(
            gram.at[pl.ds((f + 1) * modes, modes)],
            gram_near.at[slot],
            gram_send.at[f],
            gram_recv.at[slot],
            f,
            slot,
        )

    def near_copy(step, offset, sign):
        place = (2 + sign * offset[0], 2 + sign * offset[1])
        return pltpu.make_async_remote_copy(
            src_ref=coarse.at[step],
            dst_ref=coarse_near.at[step, *place],
            send_sem=near_send.at[step, *place],
            recv_sem=near_recv.at[step, *place],
            device_id=(a + offset[0], b + offset[1]),
            device_id_type=MESH,
        )

    def near_each(step, sign, what):
        for offset in around(step):

            @pl.when(inside(offset))
            def _():
                getattr(near_copy(step, offset, sign), what)()

    def gather_copy(step, k):
        return pltpu.make_async_remote_copy(
            src_ref=gathered.at[step, a],
            dst_ref=gathered.at[step, a],
            send_sem=gather_send.at[step, k],
            recv_sem=gather_recv.at[step, k],
            device_id=(lax.rem(a + k, nx), b),
            device_id_type=MESH,
        )

    def slice_copy(step, k):
        target = lax.rem(b + k, ny)
        return pltpu.make_async_remote_copy(
            src_ref=slices.at[step, target],
            dst_ref=arrived.at[step, k],
            send_sem=slice_send.at[step, k],
            recv_sem=slice_recv.at[step, k],
            device_id=(a, target),
            device_id_type=MESH,
        )

    def send(make, step, f):
        @pl.when(present[f])
        def _():
            make(step, f, opposite[f]).start()

    def sent(make, step, f):
        @pl.when(present[f])
        def _():
            make(step, f, opposite[f]).wait_send()

    def expect(make, step, f):
        @pl.when(present[f])
        def _():
            make(step, f, f).wait_recv()

    def dot(x, y):
        return jnp.dot(x, y, preferred_element_type=F32)

    def with_near(step):
        return [block(step, at) for at in ((0, 0), *compass)]

    def block(step, at):
        if at == (0, 0):
            return coarse[step]
        return coarse_near[step, 2 + at[0], 2 + at[1]]

    def with_far(step):
        blocks = []
        for centre in compass:
            for at in ((0, 0), *compass):
                blocks.append(block(step, (centre[0] + at[0], centre[1] + at[1])))
        return jnp.concatenate(blocks, axis=0)

    def share(step, total):
        gathered[step, a] = total.astype(BF16)
        for k in range(1, nx):
            gather_copy(step, k).start()

    def spread_tiles(step):
        for k in range(1, nx):
            gather_copy(step, k).wait_recv()
        partial = dot(tile[...], gathered[step].reshape(nx * modes, cols))
        slices[step] = partial.astype(BF16).reshape(ny, modes, cols)
        for k in range(1, ny):
            slice_copy(step, k).start()

    def finish_coarse(step):
        total = slices[step, b].astype(F32)
        for k in range(1, ny):
            slice_copy(step, k).wait_recv()
            total += arrived[step, k].astype(F32)
        coarse[step] = total.astype(BF16)
        near_each(step, -1, "start")

    def apply_dual(first, count):
        span = width // 2

        @pl.loop(first, first + count)
        def _(part):
            start = pl.multiple_of(part * span, span)
            base[pl.ds(start, span), :] = loads[pl.ds(start, span), :] - dot(
                dual[pl.ds(start, span), :], half[...]
            )

    def to_modes(step):
        own = jnp.zeros((modes, cols), F32)
        for f in range(4):
            both = dot(spread_rows[f], base[rows(f), :].astype(BF16))
            own += both[:modes]
            offered[step, f] = both[modes:].astype(BF16)
            send(offer_copy, step, f)
        base_modes[...] = own

    def correct(step, f):
        stacked = jnp.concatenate([coarse[step], block(step, compass[f])], axis=0)
        return DAMPING * dot(spread[rows(f), :], stacked)

    for f in range(4):
        send(face_copy, 0, f)
    for f in range(4):
        send(basis_copy, 0, f)
    total = jnp.zeros((modes, cols), F32)
    for f in range(4):
        expect(face_copy, 0, f)
        value = loads[rows(f), :] - halo[0, f].astype(F32)
        total += dot(basis[:, rows(f)], value.astype(BF16))
        out[rows(f), :] = DAMPING * value
        half[rows(f), :] = (DAMPING * value).astype(BF16)
    share(0, total)
    for f in range(4):
        expect(basis_copy, 0, f)
        pair = jnp.concatenate([basis[:, rows(f)], -beside_basis[f]], axis=0)
        spread_rows[f] = pair
        spread[rows(f), :] = pair.astype(F32).T.astype(BF16)
    dual_copy.wait()
    tile_copy.wait()
    spread_tiles(0)

    @pl.loop(0, 8)
    def _(part):
        span = width // 2
        start = pl.multiple_of(part * span, span)
        own = jnp.zeros((span, modes), F32)
        columns = []
        for f in range(4):
            both = dot(dual[pl.ds(start, span), rows(f)], spread[rows(f), :])
            own += both[:, :modes]
            columns.append(both[:, modes:])
        image[pl.ds(start, span), :] = jnp.concatenate([own] + columns, axis=1).astype(BF16)

    finish_coarse(0)
    own = jnp.zeros((modes, 5 * modes), F32)
    for f in range(4):
        both = dot(spread_rows[f], image[rows(f), :])
        own += both[:modes]
        gram[pl.ds((f + 1) * modes, modes), :] = both[modes:].astype(BF16)
    gram[pl.ds(0, modes), :] = own.astype(BF16)
    for f in range(4):
        send(gram_copy, 0, f)
    apply_dual(0, 8)
    to_modes(0)

    for step in range(1, ITERS):
        total = base_modes[...]
        for f in range(4):
            expect(offer_copy, step - 1, f)
            total += offers[step - 1, f].astype(F32)
            if step == 1:
                expect(gram_copy, 0, f)
        near_each(step - 1, 1, "wait_recv")
        stack = jnp.concatenate(with_near(step - 1), axis=0)
        change = dot(gram[pl.ds(0, modes), :], stack)
        beside = jnp.concatenate([gram_near[f] for f in range(4)], axis=1)
        change += dot(beside, with_far(step - 1))
        share(step, total + DAMPING * change)
        for f in range(4):
            value = base[rows(f), :] + DAMPING * dot(image[rows(f), :], stack)
            resid[rows(f), :] = value
            faces[step, f] = value.astype(BF16)
            send(face_copy, step, f)
        for f in range(4):
            out[rows(f), :] = out[rows(f), :] - correct(step - 1, f)
        spread_tiles(step)
        for f in range(4):
            expect(face_copy, step, f)
            value = out[rows(f), :] + DAMPING * (resid[rows(f), :] - halo[step, f].astype(F32))
            out[rows(f), :] = value
            if step < ITERS - 1:
                half[rows(f), :] = value.astype(BF16)
        if step < ITERS - 1:
            apply_dual(0, 4)
        finish_coarse(step)
        if step < ITERS - 1:
            apply_dual(4, 4)
            to_modes(step)

    near_each(ITERS - 1, 1, "wait_recv")
    for f in range(4):
        out[rows(f), :] = out[rows(f), :] - correct(ITERS - 1, f)

    for f in range(4):
        sent(basis_copy, 0, f)
        for step in range(ITERS):
            sent(face_copy, step, f)
            if step < ITERS - 1:
                sent(offer_copy, step, f)
        sent(gram_copy, 0, f)
    for step in range(ITERS):
        near_each(step, -1, "wait_send")
        for k in range(1, nx):
            gather_copy(step, k).wait_send()
        for k in range(1, ny):
            slice_copy(step, k).wait_send()


def local(nx, ny, dual_ops, loads, kernel_basis, coarse_inverse):
    n, cols = loads.shape[2:]
    modes = kernel_basis.shape[2]
    width = n // 4
    dma = pltpu.SemaphoreType.DMA
    result = pl.pallas_call(
        functools.partial(iterate, nx, ny),
        out_shape=jax.ShapeDtypeStruct((n, cols), F32),
        in_specs=[pl.BlockSpec(memory_space=pl.ANY)] * 4,
        out_specs=pl.BlockSpec(memory_space=pltpu.VMEM),
        scratch_shapes=[
            pltpu.VMEM((n, n), BF16),
            pltpu.VMEM((n, cols), F32),
            pltpu.VMEM((modes, n), BF16),
            pltpu.VMEM(coarse_inverse.shape[2:], BF16),
            pltpu.VMEM((ITERS, 4, width, cols), BF16),
            pltpu.VMEM((ITERS, 4, width, cols), BF16),
            pltpu.VMEM((4, modes, width), BF16),
            pltpu.VMEM((n, 2 * modes), BF16),
            pltpu.VMEM((4, 2 * modes, width), BF16),
            pltpu.VMEM((n, 5 * modes), BF16),
            pltpu.VMEM((5 * modes, 5 * modes), BF16),
            pltpu.VMEM((4, modes, 5 * modes), BF16),
            pltpu.VMEM((n, cols), BF16),
            pltpu.VMEM((n, cols), F32),
            pltpu.VMEM((n, cols), F32),
            pltpu.VMEM((modes, cols), F32),
            pltpu.VMEM((ITERS, 4, modes, cols), BF16),
            pltpu.VMEM((ITERS, 4, modes, cols), BF16),
            pltpu.VMEM((ITERS, nx, modes, cols), BF16),
            pltpu.VMEM((ITERS, ny, modes, cols), BF16),
            pltpu.VMEM((ITERS, ny, modes, cols), BF16),
            pltpu.VMEM((ITERS, modes, cols), BF16),
            pltpu.VMEM((ITERS, 5, 5, modes, cols), BF16),
            dma((4,)),
            dma((ITERS, 4)),
            dma((ITERS, 4)),
            dma((4,)),
            dma((4,)),
            dma((ITERS, 4)),
            dma((ITERS, 4)),
            dma((ITERS, nx)),
            dma((ITERS, nx)),
            dma((ITERS, ny)),
            dma((ITERS, ny)),
            dma((ITERS, 5, 5)),
            dma((ITERS, 5, 5)),
            dma((4,)),
            dma((4,)),
        ],
        compiler_params=pltpu.CompilerParams(
            collective_id=0, has_side_effects=True, vmem_limit_bytes=58 * 2**20
        ),
    )(dual_ops[0, 0], loads[0, 0], kernel_basis[0, 0], coarse_inverse[0, 0])
    return result[None, None]


def solution(mesh):
    placed = P("sx", "sy", None, None)
    return jax.shard_map(
        functools.partial(local, mesh.shape["sx"], mesh.shape["sy"]),
        mesh=mesh,
        in_specs=(placed,) * 4,
        out_specs=placed,
        check_vma=False,
    )
```
